32 devices in a mesh: section: 4 (over z), neuron: 8 (over y, x, core).
Axes of the slice: x: 2, y: 2, z: 4, core: 2. Of those that a mesh axis runs over, the one named last changes fastest.
Arguments:
- inputs: bfloat16 [2, 256, 16384], P(None, None, 'neuron'), may hold values from -6 to 6
- weights: bfloat16 [8, 128, 3, 128, 128], P('section', 'neuron'), may hold values from -0.4375 to 0.4375
- bias: bfloat16 [8, 16384], P('section', 'neuron'), may hold values from -0.19921875 to 0.19921875
- offsets: int32 [8, 3], P('section'), may hold values from -3 to 3, as said below
Outputs:
- outputs: bfloat16 [2, 256, 16384], P(None, 'section', 'neuron')
The draws below stay inside these ranges and needn't reach their ends.
Inputs may be any that keep to these rules, and one draw needn't show every extreme that they name: `offsets`: band 0 has offset 0; band 1 lies in 1 .. 3 and band 2 in -3 .. -1; some layer has 3 in band 1 and some layer -3 in band 2.
All inputs are finite; a program needn't handle non-finite values.
Results may differ from the reference program's by a relative error of at most 0.029.
Values may be sent and summed in bfloat16 or wider, within the bound.
No kernel may reach another device: no remote copies, remote signals or barrier semaphores. Data moves between devices by JAX's collectives and lax.ppermute only.
A program may use at most 128 MiB of HBM per device.

```python
import jax
import jax.numpy as jnp
from jax import lax

BLOCK = 128
BANDS = 3
HALO = 3
MICRO = 2
ROWS = 256
NBLOCKS = 128
NEURONS = 16384
LAYERS = 8


def draw_offsets(key, part):
    key_upward = jax.random.fold_in(key, 11)
    key_downward = jax.random.fold_in(key, 12)
    key_chosen = jax.random.fold_in(key, 13)
    upward = jax.random.randint(key_upward, (LAYERS,), 1, HALO + 1)
    downward = 0 - jax.random.randint(key_downward, (LAYERS,), 1, HALO + 1)
    chosen = jax.random.randint(key_chosen, (2,), 0, LAYERS)
    upward = upward.at[chosen[0]].set(HALO)
    downward = downward.at[chosen[1]].set(0 - HALO)
    center = jnp.zeros((LAYERS,), jnp.int32)
    return jnp.stack([center, upward.astype(jnp.int32), downward.astype(jnp.int32)], axis=1).astype(jnp.int32)


def levels(own_key, extent, shards, low, top_value):
    gain, own = 1.0, jax.random.fold_in(own_key, 6)
    for position, blocks in shards:
        steps = jnp.exp(jax.random.uniform(jax.random.fold_in(own, position), (blocks,), jnp.float32, low / len(shards), top_value / len(shards)))
        gain = gain * jnp.repeat(steps, extent[position] // blocks).reshape([-1 if axis == position else 1 for axis in range(len(extent))])
    return gain


def gaussian(rng, dims, deviation, most, cuts=(), held_as=jnp.bfloat16):
    factor_of = levels(rng, dims, cuts, -0.22, 0.18) if cuts else 1.0
    drawn = jax.random.normal(rng, dims, jnp.float32) * deviation * factor_of
    return jnp.minimum(jnp.maximum(drawn, -most), most).astype(held_as)


def setup_inputs(seed: int = 0) -> dict:
    splits = jax.random.split(jax.random.key(seed), 5)
    return {
        "inputs": gaussian(splits[0], (MICRO, ROWS, NEURONS), 1.0, 6.0, ((2, 8),)),
        "weights": gaussian(splits[1], (LAYERS, NBLOCKS, BANDS, BLOCK, BLOCK), (BANDS * BLOCK // 2) ** -0.5, 0.4375, ((0, 4), (1, 8))),
        "bias": jnp.clip(jax.random.uniform(splits[2], (LAYERS, NEURONS), jnp.float32, -0.19921875, 0.19921875) * levels(splits[2], (LAYERS, NEURONS), ((0, 4), (1, 8)), -0.4, 0.0), -0.19921875, 0.19921875).astype(jnp.bfloat16),
        "offsets": draw_offsets(jax.random.fold_in(splits[4], 71), 0),
    }


ceiling = 2.0


def reference(inputs, weights, bias, offsets):
    current = inputs
    micro_count, row_count, neuron_count = inputs.shape
    block_count = neuron_count // BLOCK
    for layer in range(LAYERS):
        summed = jnp.zeros((micro_count, row_count, block_count, BLOCK), jnp.float32)
        for band_index in range(BANDS):
            amount = (0 - offsets[layer, band_index] * BLOCK).astype(jnp.int32)
            moved = jnp.roll(current, amount, axis=2).reshape(micro_count, row_count, block_count, BLOCK).astype(jnp.float32)
            block_weights = weights[layer, :, band_index].astype(jnp.float32)
            summed = summed + jnp.einsum("mrjk,jkn->mrjn", moved, block_weights, precision=lax.Precision.HIGHEST)
        preact = summed.reshape(micro_count, row_count, neuron_count) + bias[layer].astype(jnp.float32)
        current = jnp.clip(preact, 0.0, ceiling).astype(jnp.bfloat16)
    return current
```

```python
import jax
import jax.numpy as jnp
from jax import lax
from jax.experimental import pallas as pl
from jax.experimental.pallas import tpu as pltpu
from jax.sharding import PartitionSpec as P

HALO = 3
CEILING = 2.0
CHUNK_ROWS = 32
LAG = 3


def layers_kernel(sizes, step, chunks, *refs):
    layer_count, block_count, band_count, block, margin = sizes
    where_ref, offsets_ref, bias_ref, weights_ref = refs[:4]
    margin_refs = refs[4 : 4 + 2 * (layer_count - 1)]
    refs = refs[4 + 2 * (layer_count - 1) :]
    own_ref, own_before_ref, own_after_ref = refs[:3]
    before_ref, low_ref, mid_ref, high_ref, after_ref = refs[3:8]
    out_low_ref, out_mid_ref, out_high_ref, out_ref = refs[8:12]
    buffers = refs[12:]
    section = where_ref[0]
    chunk = step - LAG * section
    edge = margin * block
    width = block_count * block

    @pl.when(jnp.logical_and(chunk >= 0, chunk < chunks))
    def _():
        first = buffers[0]

        @pl.when(section == 0)
        def _():
            first[:, :edge] = own_before_ref[...]
            first[:, edge : edge + width] = own_ref[0]
            first[:, edge + width :] = own_after_ref[...]

        @pl.when(section != 0)
        def _():
            first[:, :edge] = before_ref[...]
            first[:, edge : 2 * edge] = low_ref[...]
            first[:, 2 * edge : width] = mid_ref[...]
            first[:, width : edge + width] = high_ref[...]
            first[:, edge + width :] = after_ref[...]

        bias = bias_ref[...].astype(jnp.float32)
        for layer in range(layer_count):
            side = (layer_count - 1 - layer) * HALO
            source = buffers[layer]
            shift = [offsets_ref[layer, band] for band in range(band_count)]
            for j in range(block_count + 2 * side):
                own = j - side
                x = jnp.concatenate(
                    [
                        source[:, pl.ds(pl.multiple_of((j + HALO + s) * block, block), block)]
                        for s in shift
                    ],
                    axis=1,
                )
                depth = band_count * block
                if own < 0 or own >= block_count:
                    table = margin_refs[2 * layer + (own >= block_count)]
                    k = j if own < 0 else own - block_count
                    w = table[k * depth : (k + 1) * depth]
                    b = table[side * depth : side * depth + 16].astype(jnp.float32)[k : k + 1]
                else:
                    w = weights_ref[layer, own].reshape(depth, block)
                    b = bias[layer : layer + 1, own * block : (own + 1) * block]
                y = jnp.dot(x, w, preferred_element_type=jnp.float32) + b
                y = jnp.clip(y, 0.0, CEILING).astype(jnp.bfloat16)
                if layer < layer_count - 1:
                    buffers[layer + 1][:, j * block : (j + 1) * block] = y
                else:
                    out_ref[:, j * block : (j + 1) * block] = y
                    if j < margin:
                        out_low_ref[:, j * block : (j + 1) * block] = y
                    elif j < block_count - margin:
                        out_mid_ref[:, (j - margin) * block : (j - margin + 1) * block] = y
                    else:
                        k = j - (block_count - margin)
                        out_high_ref[:, k * block : (k + 1) * block] = y


def shards(inputs, weights, bias, offsets):
    sections = lax.axis_size("section")
    neurons = lax.axis_size("neuron")
    both = ("section", "neuron")
    section = lax.axis_index("section")
    batches, rows, width = inputs.shape
    layer_count, block_count, band_count, block, _ = weights.shape
    margin = layer_count * HALO
    edge = margin * block
    share = rows // sections
    chunk_rows = min(CHUNK_ROWS, share)
    places = [
        (batch, target * share + part * chunk_rows)
        for target in range(sections)
        for batch in range(batches)
        for part in range(share // chunk_rows)
    ]
    chunks = len(places)
    per_section = chunks // sections

    def sideways(value, which, step):
        pairs = [
            (s * neurons + n, s * neurons + (n + step) % neurons)
            for s in which
            for n in range(neurons)
        ]
        return lax.ppermute(value, both, pairs)

    def active(step):
        return [s for s in range(sections) if 0 <= step - LAG * s < chunks]

    tables = []
    for layer in range(layer_count - 1):
        side = (layer_count - 1 - layer) * HALO
        for lo, hi, step in ((block_count - side, block_count, 1), (0, side, -1)):
            b = bias[layer, lo * block : hi * block].reshape(side, block)
            b = jnp.pad(b, ((0, 16 - side), (0, 0)))
            table = jnp.concatenate([weights[layer, lo:hi].reshape(-1, block), b], axis=0)
            tables.append(sideways(table, range(sections), step))

    def input_edges(picked):
        x = jnp.concatenate(
            [inputs[b, r : r + chunk_rows] for b, r in picked], axis=0
        )
        return (
            sideways(x[:, -edge:], [0], 1),
            sideways(x[:, :edge], [0], -1),
        )

    first_edges = input_edges(places[:1])
    rest_edges = input_edges(places[1:])

    where = section.astype(jnp.int32).reshape(1)
    sizes = (layer_count, block_count, band_count, block, margin)
    smem = pl.BlockSpec(memory_space=pltpu.SMEM)
    vmem = pl.BlockSpec(memory_space=pltpu.VMEM)
    bf16 = jnp.bfloat16
    inner = width - 2 * edge

    def run(step, edges, at, pieces):
        batch, row = places[min(step, chunks - 1)]
        row_block = row // chunk_rows
        in_specs = [smem, smem, vmem, vmem] + [vmem] * len(tables)
        in_specs.append(
            pl.BlockSpec((1, chunk_rows, width), lambda i: (batch, row_block, 0))
        )
        in_specs += [pl.BlockSpec((chunk_rows, edge), lambda i: (at, 0))] * 2
        in_specs += [vmem] * 5
        widths = (edge, inner, edge, width)
        scratch = [pltpu.VMEM((chunk_rows, width + 2 * edge), bf16)]
        for layer in range(1, layer_count):
            side = (layer_count - layer) * HALO
            scratch.append(pltpu.VMEM((chunk_rows, width + 2 * side * block), bf16))
        return pl.pallas_call(
            lambda *refs: layers_kernel(sizes, step, chunks, *refs),
            grid=(1,),
            in_specs=in_specs,
            out_specs=[vmem] * 4,
            out_shape=[jax.ShapeDtypeStruct((chunk_rows, w), bf16) for w in widths],
            scratch_shapes=scratch,
            compiler_params=pltpu.CompilerParams(vmem_limit_bytes=40 * 1024 * 1024),
        )(where, offsets, bias, weights, *tables, inputs, *edges, *pieces)

    zeros = [jnp.zeros((chunk_rows, w), bf16) for w in (edge, edge, inner, edge, edge)]
    hops = {}
    returned = []
    kept = []
    for step in range(chunks + LAG * (sections - 1)):
        if step < LAG:
            pieces = zeros
        else:
            low, mid, high = hops[step - LAG]
            which = [s for s in active(step) if s > 0]
            before = sideways(high, which, 1)
            after = sideways(low, which, -1)
            pieces = [before, low, mid, high, after]
        at = min(step, chunks - 1)
        edges, at = (first_edges, 0) if at == 0 else (rest_edges, at - 1)
        out_low, out_mid, out_high, out = run(step, edges, at, pieces)
        pairs = [
            (s * neurons + n, (s + 1) * neurons + n)
            for s in active(step)
            if s + 1 < sections
            for n in range(neurons)
        ]
        if pairs:
            hops[step] = [lax.ppermute(v, both, pairs) for v in (out_low, out_mid, out_high)]
        done = step - LAG * (sections - 1)
        if done >= 0:
            target = done // per_section
            if target == sections - 1:
                kept.append(out)
            else:
                back = [
                    ((sections - 1) * neurons + n, target * neurons + n) for n in range(neurons)
                ]
                returned.append(lax.ppermute(out, both, back))

    results = []
    for k in range(per_section):
        value = returned[k]
        for target in range(1, sections - 1):
            value = value + returned[target * per_section + k]
        results.append(jnp.where(section == sections - 1, kept[k], value))
    return jnp.concatenate(results, axis=0).reshape(batches, share, width)


def solution(mesh):
    in_specs = (
        P(None, None, "neuron"),
        P("section", "neuron", None, None, None),
        P("section", "neuron"),
        P("section", None),
    )
    out_specs = P(None, "section", "neuron")
    return jax.shard_map(shards, mesh=mesh, in_specs=in_specs, out_specs=out_specs, check_vma=False)
```

```python
import jax
import jax.numpy as jnp
from jax import lax
from jax.experimental import pallas as pl
from jax.experimental.pallas import tpu as pltpu
from jax.sharding import PartitionSpec as P

HALO = 3
CEILING = 2.0
LAG = 3


def tie(value, *after):
    return lax.optimization_barrier((value, *after))[0]


def stage_kernel(copies, bias_rows, bias_ref, weights_ref, inputs_ref, where_ref, *refs):
    outs, (sems,) = refs[:-1], refs[-1:]
    sources = {"weights": weights_ref, "inputs": inputs_ref}

    def run(side):
        started = []
        for k, (out, rows, name, index) in enumerate(copies[side]):
            target = outs[out].at[rows] if rows is not None else outs[out]
            started.append(pltpu.make_async_copy(sources[name].at[index], target, sems.at[k]))
            started[-1].start()
        for out, row, layer, first, count, block in bias_rows[side]:
            own = bias_ref[layer : layer + 1, first * block : (first + count) * block]
            own = own.astype(jnp.float32)
            parts = [own[:, k * block : (k + 1) * block] for k in range(count)]
            parts.append(jnp.zeros((16 - count, block), jnp.float32))
            outs[out][row : row + 16] = jnp.concatenate(parts, axis=0).astype(jnp.bfloat16)
        for copy in started:
            copy.wait()

    if len(copies) == 1:
        run(0)
    else:

        @pl.when(where_ref[1] == 0)
        def _():
            run(0)

        @pl.when(where_ref[1] != 0)
        def _():
            run(1)


def layers_kernel(sizes, step, chunks, halo_row, *refs):
    layer_count, block_count, band_count, block, margin, share = sizes
    where_ref, offsets_ref, bias_ref, weights_ref = refs[:4]
    table_refs = refs[4 : 4 + 2 * (layer_count - 1)]
    source_ref, near_ref, far_ref, out_ref = refs[4 + 2 * (layer_count - 1) :][:4]
    buffers = refs[8 + 2 * (layer_count - 1) :]
    even = where_ref[1] == 0
    chunk = step - LAG * where_ref[0]
    edge = margin * block
    width = block_count * block
    depth = band_count * block
    rows = pl.ds(halo_row, share)

    @pl.when(jnp.logical_and(chunk >= 0, chunk < chunks))
    def _():
        first = buffers[0]
        near, far = near_ref[rows, :], far_ref[rows, :]
        first[:, :edge] = jnp.where(even, far, near)
        first[:, edge + width :] = jnp.where(even, near, far)
        first[:, edge : edge + width] = source_ref[...].reshape(share, width)

        bias = bias_ref[...].astype(jnp.float32)
        for layer in range(layer_count):
            side = (layer_count - 1 - layer) * HALO
            source = buffers[layer]
            shift = [offsets_ref[layer, band] for band in range(band_count)]
            if side:
                tables = table_refs[2 * layer : 2 * layer + 2]
                last = slice(side * depth, side * depth + 16)
                sides = [table[last].astype(jnp.float32) for table in tables]
                before_bias = jnp.where(even, sides[1], sides[0])
                after_bias = jnp.where(even, sides[0], sides[1])
            for j in range(block_count + 2 * side):
                own = j - side
                x = jnp.concatenate(
                    [
                        source[:, pl.ds(pl.multiple_of((j + HALO + s) * block, block), block)]
                        for s in shift
                    ],
                    axis=1,
                )
                if own < 0:
                    k = slice(j * depth, (j + 1) * depth)
                    w = jnp.where(even, tables[1][k], tables[0][k])
                    b = before_bias[j : j + 1]
                elif own >= block_count:
                    k = own - block_count
                    b = after_bias[k : k + 1]
                    k = slice(k * depth, (k + 1) * depth)
                    w = jnp.where(even, tables[0][k], tables[1][k])
                else:
                    w = weights_ref[layer, own].reshape(depth, block)
                    b = bias[layer : layer + 1, own * block : (own + 1) * block]
                y = jnp.dot(x, w, preferred_element_type=jnp.float32) + b
                y = jnp.clip(y, 0.0, CEILING).astype(jnp.bfloat16)
                if layer < layer_count - 1:
                    buffers[layer + 1][:, j * block : (j + 1) * block] = y
                else:
                    out_ref[:, j * block : (j + 1) * block] = y


def shards(inputs, weights, bias, offsets):
    sections = lax.axis_size("section")
    neurons = lax.axis_size("neuron")
    both = ("section", "neuron")
    section = lax.axis_index("section")
    odd = lax.axis_index("neuron") % 2
    even = odd == 0
    batches, rows, width = inputs.shape
    layer_count, block_count, band_count, block, _ = weights.shape
    margin = layer_count * HALO
    edge = margin * block
    share = rows // sections
    depth = band_count * block
    places = [(batch, target) for target in range(sections) for batch in range(batches)]
    chunks = len(places)
    assert chunks <= sections * LAG and neurons % 2 == 0 and chunks >= LAG

    near_pairs = [
        (s * neurons + n, s * neurons + (n ^ 1)) for s in range(sections) for n in range(neurons)
    ]
    far_pairs = [
        (s * neurons + n, s * neurons + (n + (1 if n % 2 else -1)) % neurons)
        for s in range(sections)
        for n in range(neurons)
    ]

    def send_near(value):
        return lax.ppermute(value, both, near_pairs)

    def send_far(value):
        return lax.ppermute(value, both, far_pairs)

    where = jnp.stack([section, odd]).astype(jnp.int32)
    sizes = (layer_count, block_count, band_count, block, margin, share)
    smem = pl.BlockSpec(memory_space=pltpu.SMEM)
    vmem = pl.BlockSpec(memory_space=pltpu.VMEM)
    hbm = pl.BlockSpec(memory_space=pltpu.HBM)
    bf16 = jnp.bfloat16
    limit = pltpu.CompilerParams(vmem_limit_bytes=12 * 1024 * 1024)

    def away(value):
        return pltpu.with_memory_space_constraint(value, pltpu.HBM)

    def stage(copies, bias_rows, shapes):
        return pl.pallas_call(
            lambda *refs: stage_kernel(copies, bias_rows, *refs),
            in_specs=[vmem, hbm, hbm, smem],
            out_specs=[vmem] * len(shapes),
            out_shape=[pltpu.VMEM(shape, bf16) for shape in shapes],
            scratch_shapes=[pltpu.SemaphoreType.DMA((max(map(len, copies)),))],
            compiler_params=limit,
        )(bias, away(weights.reshape(layer_count, block_count * depth, block)), away(inputs), where)

    ends = (pl.ds(0, edge), pl.ds(width - edge, edge))
    copies, bias_rows, shapes = [[], []], [[], []], []
    for layer in range(layer_count - 1):
        side = (layer_count - 1 - layer) * HALO
        for far in (False, True):
            for parity in range(2):
                first = 0 if far == (parity == 0) else block_count - side
                index = (layer, pl.ds(first * depth, side * depth))
                copies[parity].append((len(shapes), pl.ds(0, side * depth), "weights", index))
                bias_rows[parity].append((len(shapes), side * depth, layer, first, side, block))
            shapes.append((side * depth + 16, block))
    for steps in ((0,), range(1, LAG)):
        for far in (False, True):
            for parity in range(2):
                end = ends[0 if far == (parity == 0) else 1]
                for k, step in enumerate(steps):
                    batch, target = places[step]
                    index = (batch, pl.ds(target * share, share), end)
                    copies[parity].append((len(shapes), pl.ds(k * share, share), "inputs", index))
            shapes.append((len(steps) * share, edge))
    packed = stage(copies, bias_rows, shapes)
    tables = []
    first_halo = [send_far(packed[-3])]
    for layer in range(layer_count - 1):
        far = send_far(packed[2 * layer + 1])
        tables += [send_near(packed[2 * layer]), far]
    first_halo.insert(0, send_near(packed[-4]))
    early_far = send_far(packed[-1])
    early_halo = [send_near(packed[-2]), early_far]
    chunk_shape = (chunks, share, width)
    copies = [
        (0, k, "inputs", (batch, pl.ds(target * share, share)))
        for k, (batch, target) in enumerate(places)
    ]
    (staged,) = stage([copies], [[]], [chunk_shape])

    outputs = sum(block_count + 2 * k * HALO for k in range(layer_count))
    cost = pl.CostEstimate(
        flops=2 * outputs * share * depth * block,
        bytes_accessed=2 * (outputs * depth * block + 4 * share * width),
        transcendentals=0,
    )

    def run(step, halo_row, source, halo):
        scratch = [pltpu.VMEM((share, width + 2 * edge), bf16)]
        for layer in range(1, layer_count):
            side = (layer_count - layer) * HALO
            scratch.append(pltpu.VMEM((share, width + 2 * side * block), bf16))
        return pl.pallas_call(
            lambda *refs: layers_kernel(sizes, step, chunks, halo_row, *refs),
            in_specs=[smem, smem] + [vmem] * (5 + len(tables)),
            out_specs=vmem,
            out_shape=jax.ShapeDtypeStruct((share, width), bf16),
            scratch_shapes=scratch,
            compiler_params=limit,
            cost_estimate=cost,
        )(where, offsets, bias, weights, *tables, source, *halo)

    last = sections - 1

    def hop(step, out):
        moves = [(s, s + 1) for s in range(last) if 0 <= step - LAG * s < chunks]
        done = step - LAG * last
        if done >= 0 and places[done][1] < last:
            moves.append((last, places[done][1]))
        idle = [s for s in range(sections) if s not in [a for a, _ in moves]]
        open_ = [s for s in range(sections) if s not in [b for _, b in moves]]
        pairs = [(a * neurons + n, b * neurons + n) for a, b in moves for n in range(neurons)]
        for a, b in zip(
            [s for s in idle if s not in open_] + [s for s in idle if s in open_],
            [s for s in open_ if s not in idle] + [s for s in open_ if s in idle],
        ):
            pairs += [
                (a * neurons + n, b * neurons + (n ^ 1 if a == b else n)) for n in range(neurons)
            ]
        return lax.ppermute(out, both, pairs)

    steps = chunks + LAG * last
    hops, halos, sources, kept = {}, {}, {}, {}
    for step in range(steps):
        if step < LAG:
            source = staged[step]
            halo, halo_row = (early_halo, (step - 1) * share) if step else (first_halo, 0)
        else:
            source, halo, halo_row = sources[step], halos[step], 0
        coming = step + LAG - 2
        if coming in halos:
            source = tie(source, *halo, *sources[coming, "edges"])
        out = run(step, halo_row, source, halo)
        done = step - LAG * last
        if done < 0 or places[done][1] < last:
            hops[step] = hop(step, out)
            if done >= 0:
                kept[places[done]] = hops[step]
        else:
            kept[places[done]] = out
        coming = step + LAG - 1
        if LAG <= coming < steps:
            here = tie(hops[coming - LAG], out)
            if coming < chunks:
                here = jnp.where(section == 0, staged[coming], here)
            low, high = here[:, :edge], here[:, width - edge :]
            far, near = jnp.where(even, low, high), jnp.where(even, high, low)
            sources[coming], sources[coming, "edges"] = here, (far, near)
            far = send_far(far)
            halos[coming] = [send_near(near), far]

    results = []
    for batch in range(batches):
        value = kept[batch, last]
        for target in range(last):
            value = jnp.where(section == target, kept[batch, target], value)
        results.append(value)
    return jnp.stack(results, axis=0)


def solution(mesh):
    in_specs = (
        P(None, None, "neuron"),
        P("section", "neuron", None, None, None),
        P("section", "neuron"),
        P("section", None),
    )
    out_specs = P(None, "section", "neuron")
    return jax.shard_map(shards, mesh=mesh, in_specs=in_specs, out_specs=out_specs, check_vma=False)
```

```python
import jax
import jax.numpy as jnp
from jax import lax
from jax.experimental import pallas as pl
from jax.experimental.pallas import tpu as pltpu
from jax.sharding import PartitionSpec as P

HALO = 3
CEILING = 2.0
LAG = 3
AHEAD = 2


def tie(value, *after):
    return lax.optimization_barrier((value, *after))[0]


def in_hbm(value):
    return pltpu.with_memory_space_constraint(value, pltpu.HBM)


def stage_kernel(copies, bias_rows, where_ref, bias_ref, weights_ref, inputs_ref, *refs):
    outs, bias_buffer, bias_sem, sems = refs[:-3], refs[-3], refs[-2], refs[-1]
    sources = {"weights": weights_ref, "inputs": inputs_ref}

    def run(side):
        bias_copy = pltpu.make_async_copy(bias_ref, bias_buffer, bias_sem)
        bias_copy.start()
        started = []
        for k, (out, rows, name, index) in enumerate(copies[side]):
            target = outs[out].at[rows]
            started.append(pltpu.make_async_copy(sources[name].at[index], target, sems.at[k]))
            started[-1].start()
        bias_copy.wait()
        for out, row, layer, first, count, block in bias_rows[side]:
            own = bias_buffer[layer : layer + 1, first * block : (first + count) * block]
            own = own.astype(jnp.float32)
            parts = [own[:, k * block : (k + 1) * block] for k in range(count)]
            parts.append(jnp.zeros((16 - count, block), jnp.float32))
            outs[out][row : row + 16] = jnp.concatenate(parts, axis=0).astype(jnp.bfloat16)
        for copy in started:
            copy.wait()

    @pl.when(where_ref[1] == 0)
    def _():
        run(0)

    @pl.when(where_ref[1] != 0)
    def _():
        run(1)


def layers_kernel(sizes, step, chunks, halo_row, next_place, final, *refs):
    layer_count, block_count, band_count, block, margin, share = sizes
    where_ref, offsets_ref, bias_ref, weights_ref = refs[:4]
    refs = refs[4:]
    table_refs, refs = refs[: 2 * (layer_count - 1)], refs[2 * (layer_count - 1) :]
    source_ref, near_ref, far_ref = refs[:3]
    refs = refs[3:]
    if next_place:
        inputs_ref, out_ref, next_ref, *buffers, sem = refs
        batch, target = next_place
        following = pltpu.make_async_copy(
            inputs_ref.at[batch, pl.ds(target * share, share)], next_ref, sem
        )
        following.start()
    elif final:
        *done_refs, last_ref, all_ref = refs[: final + 2]
        out_ref, buffers = all_ref.at[final - 1], refs[final + 2 :]
    else:
        out_ref, *buffers = refs
    even = where_ref[1] == 0
    chunk = step - LAG * where_ref[0]
    edge = margin * block
    width = block_count * block
    depth = band_count * block
    rows = pl.ds(halo_row, share)
    active = jnp.logical_and(chunk >= 0, chunk < chunks)

    @pl.when(active)
    def _():
        first = buffers[0]
        near, far = near_ref[rows, :], far_ref[rows, :]
        first[:, :edge] = jnp.where(even, far, near)
        first[:, edge + width :] = jnp.where(even, near, far)
        first[:, edge : edge + width] = source_ref[...]

        bias = bias_ref[...].astype(jnp.float32)
        for layer in range(layer_count):
            side = (layer_count - 1 - layer) * HALO
            source = buffers[layer]
            shift = [offsets_ref[layer, band] for band in range(band_count)]
            if side:
                tables = table_refs[2 * layer : 2 * layer + 2]
                last = slice(side * depth, side * depth + 16)
                sides = [table[last].astype(jnp.float32) for table in tables]
                before_bias = jnp.where(even, sides[1], sides[0])
                after_bias = jnp.where(even, sides[0], sides[1])
            for j in range(block_count + 2 * side):
                own = j - side
                x = jnp.concatenate(
                    [
                        source[:, pl.ds(pl.multiple_of((j + HALO + s) * block, block), block)]
                        for s in shift
                    ],
                    axis=1,
                )
                if own < 0:
                    k = slice(j * depth, (j + 1) * depth)
                    w = jnp.where(even, tables[1][k], tables[0][k])
                    b = before_bias[j : j + 1]
                elif own >= block_count:
                    k = own - block_count
                    b = after_bias[k : k + 1]
                    k = slice(k * depth, (k + 1) * depth)
                    w = jnp.where(even, tables[0][k], tables[1][k])
                else:
                    w = weights_ref[layer, own].reshape(depth, block)
                    b = bias[layer : layer + 1, own * block : (own + 1) * block]
                y = jnp.dot(x, w, preferred_element_type=jnp.float32) + b
                y = jnp.clip(y, 0.0, CEILING).astype(jnp.bfloat16)
                if layer < layer_count - 1:
                    buffers[layer + 1][:, j * block : (j + 1) * block] = y
                else:
                    out_ref[:, j * block : (j + 1) * block] = y

    if next_place:
        following.wait()
    if final:
        @pl.when(active)
        def _():
            for batch in range(final - 1):
                all_ref[batch] = last_ref[batch]

        @pl.when(jnp.logical_not(active))
        def _():
            for batch in range(final):
                all_ref[batch] = done_refs[batch][...]


def shards(inputs, weights, bias, offsets):
    sections = lax.axis_size("section")
    neurons = lax.axis_size("neuron")
    both = ("section", "neuron")
    section = lax.axis_index("section")
    odd = lax.axis_index("neuron") % 2
    batches, rows, width = inputs.shape
    layer_count, block_count, band_count, block, _ = weights.shape
    margin = layer_count * HALO
    edge = margin * block
    share = rows // sections
    depth = band_count * block
    places = [(batch, target) for target in range(sections) for batch in range(batches)]
    chunks = len(places)
    assert chunks <= sections * LAG and neurons % 2 == 0 and chunks > LAG

    def send_near(value):
        pairs = [
            (s * neurons + n, s * neurons + (n ^ 1))
            for s in range(sections)
            for n in range(neurons)
        ]
        return lax.ppermute(value, both, pairs)

    def send_far(value, which=range(sections)):
        pairs = []
        for s in range(sections):
            for n in range(neurons):
                other = (n + (1 if n % 2 else -1)) % neurons if s in which else n ^ 1
                pairs.append((s * neurons + n, s * neurons + other))
        return lax.ppermute(value, both, pairs)

    where = jnp.stack([section, odd]).astype(jnp.int32)
    here_is = [section == s for s in range(sections - 1)]
    even, inputs, weights, bias, offsets, where, *here_is = lax.optimization_barrier(
        (odd == 0, inputs, weights, bias, offsets, where, *here_is)
    )
    sizes = (layer_count, block_count, band_count, block, margin, share)
    smem = pl.BlockSpec(memory_space=pltpu.SMEM)
    vmem = pl.BlockSpec(memory_space=pltpu.VMEM)
    hbm = pl.BlockSpec(memory_space=pltpu.HBM)
    bf16 = jnp.bfloat16
    limit = pltpu.CompilerParams(vmem_limit_bytes=8 * 1024 * 1024)

    copies, bias_rows, shapes = [[], []], [[], []], []
    for far in (True, False):
        for parity in range(2):
            end = pl.ds(0 if far == (parity == 0) else width - edge, edge)
            for k in range(AHEAD):
                batch, target = places[k]
                index = (batch, pl.ds(target * share, share), end)
                copies[parity].append((len(shapes), pl.ds(k * share, share), "inputs", index))
        shapes.append((AHEAD * share, edge))
    for layer in range(layer_count - 1):
        side = (layer_count - 1 - layer) * HALO
        for far in (True, False):
            for parity in range(2):
                first = 0 if far == (parity == 0) else block_count - side
                index = (layer, pl.ds(first * depth, side * depth))
                copies[parity].append((len(shapes), pl.ds(0, side * depth), "weights", index))
                bias_rows[parity].append((len(shapes), side * depth, layer, first, side, block))
            shapes.append((side * depth + 16, block))
    for k in range(AHEAD):
        batch, target = places[k]
        index = (batch, pl.ds(target * share, share))
        for parity in range(2):
            copies[parity].append((len(shapes), pl.ds(0, share), "inputs", index))
        shapes.append((share, width))
    packed = pl.pallas_call(
        lambda *refs: stage_kernel(copies, bias_rows, *refs),
        in_specs=[smem, hbm, hbm, hbm],
        out_specs=[vmem] * len(shapes),
        out_shape=[pltpu.VMEM(shape, bf16) for shape in shapes],
        scratch_shapes=[
            pltpu.VMEM(bias.shape, bf16),
            pltpu.SemaphoreType.DMA,
            pltpu.SemaphoreType.DMA((len(copies[0]),)),
        ],
        compiler_params=limit,
    )(
        where,
        in_hbm(bias),
        in_hbm(weights.reshape(layer_count, block_count * depth, block)),
        in_hbm(inputs),
    )
    first_far = send_far(packed[0], [0])
    tables = []
    for layer in range(layer_count - 1):
        far = send_far(packed[2 + 2 * layer])
        tables += [send_near(packed[3 + 2 * layer]), far]
    first_halo = [send_near(packed[1]), first_far]

    def run(step, halo_row, source, halo, finished=None):
        scratch = [pltpu.VMEM((share, width + 2 * edge), bf16)]
        for layer in range(1, layer_count):
            side = (layer_count - layer) * HALO
            scratch.append(pltpu.VMEM((share, width + 2 * side * block), bf16))
        operands = [where, offsets, bias, weights, *tables, source, *halo]
        in_specs = [smem, smem] + [vmem] * (len(operands) - 2)
        out_shape = [jax.ShapeDtypeStruct((share, width), bf16)]
        next_place, final = None, 0
        if step + AHEAD < chunks:
            next_place = places[step + AHEAD]
            operands.append(in_hbm(inputs))
            in_specs.append(hbm)
            out_shape.append(pltpu.VMEM((share, width), bf16))
            scratch.append(pltpu.SemaphoreType.DMA)
        elif finished:
            final = batches
            operands += finished
            in_specs += [vmem] * len(finished)
            out_shape = [jax.ShapeDtypeStruct((batches, share, width), bf16)]
        return pl.pallas_call(
            lambda *refs: layers_kernel(sizes, step, chunks, halo_row, next_place, final, *refs),
            in_specs=in_specs,
            out_specs=[vmem] * len(out_shape),
            out_shape=out_shape,
            scratch_shapes=scratch,
            compiler_params=limit,
        )(*operands)

    last = sections - 1

    def hop(step, out):
        moves = [(s, s + 1) for s in range(last) if 0 <= step - LAG * s < chunks]
        done = step - LAG * last
        if done >= 0 and places[done][1] < last:
            moves.append((last, places[done][1]))
        idle = [s for s in range(sections) if s not in [a for a, _ in moves]]
        open_ = [s for s in range(sections) if s not in [b for _, b in moves]]
        pairs = [(a * neurons + n, b * neurons + n) for a, b in moves for n in range(neurons)]
        for a, b in zip(
            [s for s in idle if s not in open_] + [s for s in idle if s in open_],
            [s for s in open_ if s not in idle] + [s for s in open_ if s in idle],
        ):
            pairs += [
                (a * neurons + n, b * neurons + (n ^ 1 if a == b else n)) for n in range(neurons)
            ]
        return lax.ppermute(out, both, pairs)

    steps = chunks + LAG * last
    own = {k: packed[k - AHEAD] for k in range(AHEAD)}
    sources, halos, sent, hops = {}, {}, {}, {}
    finished = [None] * batches
    ended = []
    for step in range(steps):
        if step < AHEAD:
            source, halo, halo_row = own[step], first_halo, step * share
        else:
            source, halo, halo_row = sources[step], halos[step], 0
        source = tie(source, *halo, *sent.get(step + 1, ()))
        ending = step == steps - 1
        if ending:
            (result,) = run(step, halo_row, source, halo, finished + [jnp.stack(ended)])
            return result
        out, *following = run(step, halo_row, source, halo)
        if following:
            own[step + AHEAD] = following[0]
        done = step - LAG * last
        if done < 0 or places[done][1] < last:
            hops[step] = hop(step, out)
        else:
            ended.append(out)
        coming = step + AHEAD
        if coming < steps:
            after = (out, *halos.get(coming - 1, ()))
            if coming < LAG:
                here = tie(own[coming], *after)
            else:
                here = tie(hops[coming - LAG], *after)
                if coming < chunks:
                    here = jnp.where(here_is[0], own[coming], here)
            sources[coming] = here
            low, high = here[:, :edge], here[:, width - edge :]
            sent[coming] = (jnp.where(even, low, high), jnp.where(even, high, low))
            which = [s for s in range(sections) if 0 <= coming - LAG * s < chunks]
            far = send_far(sent[coming][0], which)
            halos[coming] = [send_near(sent[coming][1]), far]
        back = step - 1 - LAG * last
        if back >= 0 and places[back][1] < last:
            batch, target = places[back]
            arrived = hops[step - 1]
            if finished[batch] is not None:
                arrived = jnp.where(here_is[target], arrived, finished[batch])
            finished[batch] = arrived


def solution(mesh):
    in_specs = (
        P(None, None, "neuron"),
        P("section", "neuron", None, None, None),
        P("section", "neuron"),
        P("section", None),
    )
    out_specs = P(None, "section", "neuron")
    return jax.shard_map(shards, mesh=mesh, in_specs=in_specs, out_specs=out_specs, check_vma=False)
```

```python
import jax
import jax.numpy as jnp
from jax import lax
from jax.experimental import pallas as pl
from jax.experimental.pallas import tpu as pltpu
from jax.sharding import PartitionSpec as P

HALO = 3
CEILING = 2.0
LAG = 3
AHEAD = 2


def tie(value, *after):
    return lax.optimization_barrier((value, *after))[0]


def in_hbm(value):
    return pltpu.with_memory_space_constraint(value, pltpu.HBM)


def stage_kernel(copies, bias_rows, where_ref, bias_ref, weights_ref, inputs_ref, *refs):
    outs, bias_buffer, bias_sem, sems = refs[:-3], refs[-3], refs[-2], refs[-1]
    sources = {"weights": weights_ref, "inputs": inputs_ref}

    def run(side):
        bias_copy = pltpu.make_async_copy(bias_ref, bias_buffer, bias_sem)
        bias_copy.start()
        started = []
        for k, (out, rows, name, index) in enumerate(copies[side]):
            target = outs[out].at[rows]
            started.append(pltpu.make_async_copy(sources[name].at[index], target, sems.at[k]))
            started[-1].start()
        bias_copy.wait()
        for out, row, layer, first, count, block in bias_rows[side]:
            own = bias_buffer[layer : layer + 1, first * block : (first + count) * block]
            own = own.astype(jnp.float32)
            parts = [own[:, k * block : (k + 1) * block] for k in range(count)]
            parts.append(jnp.zeros((16 - count, block), jnp.float32))
            outs[out][row : row + 16] = jnp.concatenate(parts, axis=0).astype(jnp.bfloat16)
        for copy in started:
            copy.wait()

    @pl.when(where_ref[1] == 0)
    def _():
        run(0)

    @pl.when(where_ref[1] != 0)
    def _():
        run(1)


def layers_kernel(sizes, step, chunks, next_place, final, *refs):
    layer_count, block_count, band_count, block, margin, share = sizes
    where_ref, offsets_ref, bias_ref, weights_ref = refs[:4]
    refs = refs[4:]
    table_refs, refs = refs[: 2 * (layer_count - 1)], refs[2 * (layer_count - 1) :]
    source_ref, near_ref, far_ref = refs[:3]
    refs = refs[3:]
    if next_place:
        inputs_ref, out_ref, next_ref, *buffers, sem = refs
        batch, target = next_place
        following = pltpu.make_async_copy(
            inputs_ref.at[batch, pl.ds(target * share, share)], next_ref, sem
        )
        following.start()
    elif final:
        *done_refs, last_ref, all_ref = refs[: final + 2]
        out_ref, buffers = all_ref.at[final - 1], refs[final + 2 :]
    else:
        out_ref, *buffers = refs
    even = where_ref[1] == 0
    chunk = step - LAG * where_ref[0]
    edge = margin * block
    width = block_count * block
    depth = band_count * block
    active = jnp.logical_and(chunk >= 0, chunk < chunks)

    @pl.when(active)
    def _():
        first = buffers[0]
        near, far = near_ref[...], far_ref[...]
        first[:, :edge] = jnp.where(even, far, near)
        first[:, edge + width :] = jnp.where(even, near, far)
        first[:, edge : edge + width] = source_ref[...]

        bias = bias_ref[...].astype(jnp.float32)
        for layer in range(layer_count):
            side = (layer_count - 1 - layer) * HALO
            source = buffers[layer]
            shift = [offsets_ref[layer, band] for band in range(band_count)]
            if side:
                tables = table_refs[2 * layer : 2 * layer + 2]
                last = slice(side * depth, side * depth + 16)
                sides = [table[last].astype(jnp.float32) for table in tables]
                before_bias = jnp.where(even, sides[1], sides[0])
                after_bias = jnp.where(even, sides[0], sides[1])
            for j in range(block_count + 2 * side):
                own = j - side
                x = jnp.concatenate(
                    [
                        source[:, pl.ds(pl.multiple_of((j + HALO + s) * block, block), block)]
                        for s in shift
                    ],
                    axis=1,
                )
                if own < 0:
                    k = slice(j * depth, (j + 1) * depth)
                    w = jnp.where(even, tables[1][k], tables[0][k])
                    b = before_bias[j : j + 1]
                elif own >= block_count:
                    k = own - block_count
                    b = after_bias[k : k + 1]
                    k = slice(k * depth, (k + 1) * depth)
                    w = jnp.where(even, tables[0][k], tables[1][k])
                else:
                    w = weights_ref[layer, own].reshape(depth, block)
                    b = bias[layer : layer + 1, own * block : (own + 1) * block]
                y = jnp.dot(x, w, preferred_element_type=jnp.float32) + b
                y = jnp.clip(y, 0.0, CEILING).astype(jnp.bfloat16)
                if layer < layer_count - 1:
                    buffers[layer + 1][:, j * block : (j + 1) * block] = y
                else:
                    out_ref[:, j * block : (j + 1) * block] = y

    if next_place:
        following.wait()
    if final:
        @pl.when(active)
        def _():
            for batch in range(final - 1):
                all_ref[batch] = last_ref[batch]

        @pl.when(jnp.logical_not(active))
        def _():
            for batch in range(final):
                all_ref[batch] = done_refs[batch][...]


def shards(inputs, weights, bias, offsets):
    sections = lax.axis_size("section")
    neurons = lax.axis_size("neuron")
    both = ("section", "neuron")
    section = lax.axis_index("section")
    odd = lax.axis_index("neuron") % 2
    batches, rows, width = inputs.shape
    layer_count, block_count, band_count, block, _ = weights.shape
    margin = layer_count * HALO
    edge = margin * block
    share = rows // sections
    depth = band_count * block
    places = [(batch, target) for target in range(sections) for batch in range(batches)]
    chunks = len(places)
    assert chunks <= sections * LAG and neurons % 2 == 0 and chunks > LAG

    def send_near(value):
        pairs = [
            (s * neurons + n, s * neurons + (n ^ 1))
            for s in range(sections)
            for n in range(neurons)
        ]
        return lax.ppermute(value, both, pairs)

    def send_far(value, which=range(sections)):
        pairs = []
        for s in range(sections):
            for n in range(neurons):
                other = (n + (1 if n % 2 else -1)) % neurons if s in which else n ^ 1
                pairs.append((s * neurons + n, s * neurons + other))
        return lax.ppermute(value, both, pairs)

    where = jnp.stack([section, odd]).astype(jnp.int32)
    here_is = [section == s for s in range(sections - 1)]
    even, inputs, weights, bias, offsets, where, *here_is = lax.optimization_barrier(
        (odd == 0, inputs, weights, bias, offsets, where, *here_is)
    )
    sizes = (layer_count, block_count, band_count, block, margin, share)
    smem = pl.BlockSpec(memory_space=pltpu.SMEM)
    vmem = pl.BlockSpec(memory_space=pltpu.VMEM)
    hbm = pl.BlockSpec(memory_space=pltpu.HBM)
    bf16 = jnp.bfloat16
    limit = pltpu.CompilerParams(vmem_limit_bytes=8 * 1024 * 1024)

    copies, bias_rows, shapes = [[], []], [[], []], []
    for k in range(AHEAD):
        batch, target = places[k]
        for far in (True, False):
            for parity in range(2):
                end = pl.ds(0 if far == (parity == 0) else width - edge, edge)
                index = (batch, pl.ds(target * share, share), end)
                copies[parity].append((len(shapes), pl.ds(0, share), "inputs", index))
            shapes.append((share, edge))
    for layer in range(layer_count - 1):
        side = (layer_count - 1 - layer) * HALO
        for far in (True, False):
            for parity in range(2):
                first = 0 if far == (parity == 0) else block_count - side
                index = (layer, pl.ds(first * depth, side * depth))
                copies[parity].append((len(shapes), pl.ds(0, side * depth), "weights", index))
                bias_rows[parity].append((len(shapes), side * depth, layer, first, side, block))
            shapes.append((side * depth + 16, block))
    for k in range(AHEAD):
        batch, target = places[k]
        index = (batch, pl.ds(target * share, share))
        for parity in range(2):
            copies[parity].append((len(shapes), pl.ds(0, share), "inputs", index))
        shapes.append((share, width))
    def stage(wanted, first):
        at = {k: i for i, k in enumerate(wanted)}
        my_copies = [[(at[c[0]], *c[1:]) for c in side if c[0] in at] for side in copies]
        my_rows = [[(at[c[0]], *c[1:]) for c in side if c[0] in at] for side in bias_rows]
        return pl.pallas_call(
            lambda *refs: stage_kernel(my_copies, my_rows, *refs),
            in_specs=[smem, hbm, hbm, hbm],
            out_specs=[vmem] * len(wanted),
            out_shape=[pltpu.VMEM(shapes[k], bf16) for k in wanted],
            scratch_shapes=[
                pltpu.VMEM(bias.shape, bf16),
                pltpu.SemaphoreType.DMA,
                pltpu.SemaphoreType.DMA((len(my_copies[0]),)),
            ],
            compiler_params=limit,
        )(
            tie(where, *first),
            in_hbm(bias),
            in_hbm(weights.reshape(layer_count, block_count * depth, block)),
            in_hbm(inputs),
        )

    urgent = list(range(2 * AHEAD, 2 * AHEAD + 2 * (layer_count - 1), 2))
    packed = dict(zip(urgent, stage(urgent, ())))
    others = [k for k in range(len(shapes)) if k not in urgent]
    packed.update(zip(others, stage(others, packed.values())))
    halos = {}
    for k in range(AHEAD):
        if k == 1:
            tables = []
            for layer in range(layer_count - 1):
                far = send_far(packed[2 * AHEAD + 2 * layer])
                tables += [send_near(packed[2 * AHEAD + 1 + 2 * layer]), far]
        far = send_far(packed[2 * k], [0])
        halos[k] = [send_near(packed[2 * k + 1]), far]

    def run(step, source, halo, finished=None):
        scratch = [pltpu.VMEM((share, width + 2 * edge), bf16)]
        for layer in range(1, layer_count):
            side = (layer_count - layer) * HALO
            scratch.append(pltpu.VMEM((share, width + 2 * side * block), bf16))
        operands = [where, offsets, bias, weights, *tables, source, *halo]
        in_specs = [smem, smem] + [vmem] * (len(operands) - 2)
        out_shape = [jax.ShapeDtypeStruct((share, width), bf16)]
        next_place, final = None, 0
        if step + AHEAD < chunks:
            next_place = places[step + AHEAD]
            operands.append(in_hbm(inputs))
            in_specs.append(hbm)
            out_shape.append(pltpu.VMEM((share, width), bf16))
            scratch.append(pltpu.SemaphoreType.DMA)
        elif finished:
            final = batches
            operands += finished
            in_specs += [vmem] * len(finished)
            out_shape = [jax.ShapeDtypeStruct((batches, share, width), bf16)]
        return pl.pallas_call(
            lambda *refs: layers_kernel(sizes, step, chunks, next_place, final, *refs),
            in_specs=in_specs,
            out_specs=[vmem] * len(out_shape),
            out_shape=out_shape,
            scratch_shapes=scratch,
            compiler_params=limit,
        )(*operands)

    last = sections - 1

    def hop(step, out):
        moves = [(s, s + 1) for s in range(last) if 0 <= step - LAG * s < chunks]
        done = step - LAG * last
        if done >= 0 and places[done][1] < last:
            moves.append((last, places[done][1]))
        idle = [s for s in range(sections) if s not in [a for a, _ in moves]]
        open_ = [s for s in range(sections) if s not in [b for _, b in moves]]
        pairs = [(a * neurons + n, b * neurons + n) for a, b in moves for n in range(neurons)]
        if 0 < step <= LAG:
            idle = [s for s in idle if s in open_]
            open_ = idle
        for a, b in zip(
            [s for s in idle if s not in open_] + [s for s in idle if s in open_],
            [s for s in open_ if s not in idle] + [s for s in open_ if s in idle],
        ):
            pairs += [
                (a * neurons + n, b * neurons + (n ^ 1 if a == b else n)) for n in range(neurons)
            ]
        return lax.ppermute(out, both, pairs)

    steps = chunks + LAG * last
    own = {k: packed[len(shapes) - AHEAD + k] for k in range(AHEAD)}
    sources, sent, hops = {}, {}, {}
    finished = [None] * batches
    ended = []
    for step in range(steps):
        if step < AHEAD:
            source = own[step]
        else:
            source = sources[step]
        halo = halos[step]
        source = tie(source, *halo, *sent.get(step + 1, ()))
        ending = step == steps - 1
        if ending:
            (result,) = run(step, source, halo, finished + [jnp.stack(ended)])
            return result
        out, *following = run(step, source, halo)
        if following:
            own[step + AHEAD] = following[0]
        done = step - LAG * last
        if done < 0 or places[done][1] < last:
            hops[step] = hop(step, out)
        else:
            ended.append(out)
        coming = step + AHEAD
        if coming < steps:
            after = (out, *halos[coming - 1]) if coming < steps - 1 else (out,)
            if coming < LAG:
                here = tie(own[coming], *after)
            else:
                here = tie(hops[coming - LAG], *after)
                if coming < chunks:
                    here = jnp.where(here_is[0], own[coming], here)
            sources[coming] = here
            low, high = here[:, :edge], here[:, width - edge :]
            sent[coming] = (jnp.where(even, low, high), jnp.where(even, high, low))
            which = [s for s in range(sections) if 0 <= coming - LAG * s < chunks]
            far = send_far(sent[coming][0], which)
            halos[coming] = [send_near(sent[coming][1]), far]
        back = step - 1 - LAG * last
        if back >= 0 and places[back][1] < last:
            batch, target = places[back]
            arrived = hops[step - 1]
            if finished[batch] is not None:
                arrived = jnp.where(here_is[target], arrived, finished[batch])
            finished[batch] = arrived


def solution(mesh):
    in_specs = (
        P(None, None, "neuron"),
        P("section", "neuron", None, None, None),
        P("section", "neuron"),
        P("section", None),
    )
    out_specs = P(None, "section", "neuron")
    return jax.shard_map(shards, mesh=mesh, in_specs=in_specs, out_specs=out_specs, check_vma=False)
```

```python
import jax
import jax.numpy as jnp
from jax import lax
from jax.experimental import pallas as pl
from jax.experimental.pallas import tpu as pltpu
from jax.sharding import PartitionSpec as P

HALO = 3
CEILING = 2.0
LAG = 3
AHEAD = 2


def tie(value, *after):
    return lax.optimization_barrier((value, *after))[0]


def in_hbm(value):
    return pltpu.with_memory_space_constraint(value, pltpu.HBM)


def stage_kernel(copies, bias_rows, where_ref, bias_ref, weights_ref, inputs_ref, *refs):
    outs, bias_buffer, bias_sem, sems = refs[:-3], refs[-3], refs[-2], refs[-1]
    sources = {"weights": weights_ref, "inputs": inputs_ref}

    def run(side):
        bias_copy = pltpu.make_async_copy(bias_ref, bias_buffer, bias_sem)
        bias_copy.start()
        started = []
        for k, (out, rows, name, index) in enumerate(copies[side]):
            target = outs[out].at[rows]
            started.append(pltpu.make_async_copy(sources[name].at[index], target, sems.at[k]))
            started[-1].start()
        bias_copy.wait()
        for out, row, layer, first, count, block in bias_rows[side]:
            own = bias_buffer[layer : layer + 1, first * block : (first + count) * block]
            own = own.astype(jnp.float32)
            parts = [own[:, k * block : (k + 1) * block] for k in range(count)]
            parts.append(jnp.zeros((16 - count, block), jnp.float32))
            outs[out][row : row + 16] = jnp.concatenate(parts, axis=0).astype(jnp.bfloat16)
        for copy in started:
            copy.wait()

    @pl.when(where_ref[1] == 0)
    def _():
        run(0)

    @pl.when(where_ref[1] != 0)
    def _():
        run(1)


def layers_kernel(sizes, step, chunks, next_place, final, *refs):
    layer_count, block_count, band_count, block, margin, share = sizes
    where_ref, offsets_ref, bias_ref, weights_ref = refs[:4]
    refs = refs[4:]
    table_refs, refs = refs[: 2 * (layer_count - 1)], refs[2 * (layer_count - 1) :]
    source_ref, near_ref, far_ref = refs[:3]
    refs = refs[3:]
    if next_place:
        inputs_ref, out_ref, next_ref, *buffers, sem = refs
        batch, target = next_place
        following = pltpu.make_async_copy(
            inputs_ref.at[batch, pl.ds(target * share, share)], next_ref, sem
        )
        following.start()
    elif final:
        *done_refs, last_ref, all_ref = refs[: final + 2]
        out_ref, buffers = all_ref.at[final - 1], refs[final + 2 :]
    else:
        out_ref, *buffers = refs
    even = where_ref[1] == 0
    chunk = step - LAG * where_ref[0]
    edge = margin * block
    width = block_count * block
    depth = band_count * block
    active = jnp.logical_and(chunk >= 0, chunk < chunks)

    @pl.when(active)
    def _():
        first = buffers[0]
        near, far = near_ref[...], far_ref[...]
        first[:, :edge] = jnp.where(even, far, near)
        first[:, edge + width :] = jnp.where(even, near, far)
        first[:, edge : edge + width] = source_ref[...]

        bias = bias_ref[...].astype(jnp.float32)
        for layer in range(layer_count):
            side = (layer_count - 1 - layer) * HALO
            source = buffers[layer]
            shift = [offsets_ref[layer, band] for band in range(band_count)]
            if side:
                tables = table_refs[2 * layer : 2 * layer + 2]
                last = slice(side * depth, side * depth + 16)
                sides = [table[last].astype(jnp.float32) for table in tables]
                before_bias = jnp.where(even, sides[1], sides[0])
                after_bias = jnp.where(even, sides[0], sides[1])
            for j in range(block_count + 2 * side):
                own = j - side
                x = jnp.concatenate(
                    [
                        source[:, pl.ds(pl.multiple_of((j + HALO + s) * block, block), block)]
                        for s in shift
                    ],
                    axis=1,
                )
                if own < 0:
                    k = slice(j * depth, (j + 1) * depth)
                    w = jnp.where(even, tables[1][k], tables[0][k])
                    b = before_bias[j : j + 1]
                elif own >= block_count:
                    k = own - block_count
                    b = after_bias[k : k + 1]
                    k = slice(k * depth, (k + 1) * depth)
                    w = jnp.where(even, tables[0][k], tables[1][k])
                else:
                    w = weights_ref[layer, own].reshape(depth, block)
                    b = bias[layer : layer + 1, own * block : (own + 1) * block]
                y = jnp.dot(x, w, preferred_element_type=jnp.float32) + b
                y = jnp.clip(y, 0.0, CEILING).astype(jnp.bfloat16)
                if layer < layer_count - 1:
                    buffers[layer + 1][:, j * block : (j + 1) * block] = y
                else:
                    out_ref[:, j * block : (j + 1) * block] = y

    if next_place:
        following.wait()
    if final:
        @pl.when(active)
        def _():
            for batch in range(final - 1):
                all_ref[batch] = last_ref[batch]

        @pl.when(jnp.logical_not(active))
        def _():
            for batch in range(final):
                all_ref[batch] = done_refs[batch][...]


def shards(inputs, weights, bias, offsets):
    sections = lax.axis_size("section")
    neurons = lax.axis_size("neuron")
    both = ("section", "neuron")
    section = lax.axis_index("section")
    odd = lax.axis_index("neuron") % 2
    batches, rows, width = inputs.shape
    layer_count, block_count, band_count, block, _ = weights.shape
    margin = layer_count * HALO
    edge = margin * block
    share = rows // sections
    depth = band_count * block
    places = [(batch, target) for target in range(sections) for batch in range(batches)]
    chunks = len(places)
    assert chunks <= sections * LAG and neurons % 2 == 0 and chunks > LAG

    def send_near(value):
        pairs = [
            (s * neurons + n, s * neurons + (n ^ 1))
            for s in range(sections)
            for n in range(neurons)
        ]
        return lax.ppermute(value, both, pairs)

    def send_far(value, which=range(sections)):
        pairs = []
        for s in range(sections):
            for n in range(neurons):
                other = (n + (1 if n % 2 else -1)) % neurons if s in which else n ^ 1
                pairs.append((s * neurons + n, s * neurons + other))
        return lax.ppermute(value, both, pairs)

    where = jnp.stack([section, odd]).astype(jnp.int32)
    here_is = [section == s for s in range(sections - 1)]
    even, inputs, weights, bias, offsets, where, *here_is = lax.optimization_barrier(
        (odd == 0, inputs, weights, bias, offsets, where, *here_is)
    )
    sizes = (layer_count, block_count, band_count, block, margin, share)
    smem = pl.BlockSpec(memory_space=pltpu.SMEM)
    vmem = pl.BlockSpec(memory_space=pltpu.VMEM)
    hbm = pl.BlockSpec(memory_space=pltpu.HBM)
    bf16 = jnp.bfloat16
    limit = pltpu.CompilerParams(vmem_limit_bytes=8 * 1024 * 1024)

    copies, bias_rows, shapes = [[], []], [[], []], []
    for k in range(AHEAD):
        batch, target = places[k]
        for far in (True, False):
            for parity in range(2):
                end = pl.ds(0 if far == (parity == 0) else width - edge, edge)
                index = (batch, pl.ds(target * share, share), end)
                copies[parity].append((len(shapes), pl.ds(0, share), "inputs", index))
            shapes.append((share, edge))
    for layer in range(layer_count - 1):
        side = (layer_count - 1 - layer) * HALO
        for far in (True, False):
            for parity in range(2):
                first = 0 if far == (parity == 0) else block_count - side
                index = (layer, pl.ds(first * depth, side * depth))
                copies[parity].append((len(shapes), pl.ds(0, side * depth), "weights", index))
                bias_rows[parity].append((len(shapes), side * depth, layer, first, side, block))
            shapes.append((side * depth + 16, block))
    for k in range(AHEAD):
        batch, target = places[k]
        index = (batch, pl.ds(target * share, share))
        for parity in range(2):
            copies[parity].append((len(shapes), pl.ds(0, share), "inputs", index))
        shapes.append((share, width))
    def stage(wanted, first):
        at = {k: i for i, k in enumerate(wanted)}
        my_copies = [[(at[c[0]], *c[1:]) for c in side if c[0] in at] for side in copies]
        my_rows = [[(at[c[0]], *c[1:]) for c in side if c[0] in at] for side in bias_rows]
        return pl.pallas_call(
            lambda *refs: stage_kernel(my_copies, my_rows, *refs),
            in_specs=[smem, hbm, hbm, hbm],
            out_specs=[vmem] * len(wanted),
            out_shape=[pltpu.VMEM(shapes[k], bf16) for k in wanted],
            scratch_shapes=[
                pltpu.VMEM(bias.shape, bf16),
                pltpu.SemaphoreType.DMA,
                pltpu.SemaphoreType.DMA((len(my_copies[0]),)),
            ],
            compiler_params=limit,
        )(
            tie(where, *first),
            in_hbm(bias),
            in_hbm(weights.reshape(layer_count, block_count * depth, block)),
            in_hbm(inputs),
        )

    urgent = list(range(2 * AHEAD, 2 * AHEAD + 2 * (layer_count - 1), 2))
    packed = dict(zip(urgent, stage(urgent, ())))
    others = [k for k in range(len(shapes)) if k not in urgent]
    packed.update(zip(others, stage(others, packed.values())))
    halos = {}
    for k in range(AHEAD):
        if k == 1:
            tables = []
            for layer in range(layer_count - 1):
                far = send_far(packed[2 * AHEAD + 2 * layer])
                tables += [send_near(packed[2 * AHEAD + 1 + 2 * layer]), far]
        far = send_far(packed[2 * k], [0])
        halos[k] = [send_near(packed[2 * k + 1]), far]

    def run(step, source, halo, finished=None):
        scratch = [pltpu.VMEM((share, width + 2 * edge), bf16)]
        for layer in range(1, layer_count):
            side = (layer_count - layer) * HALO
            scratch.append(pltpu.VMEM((share, width + 2 * side * block), bf16))
        operands = [where, offsets, bias, weights, *tables, source, *halo]
        in_specs = [smem, smem] + [vmem] * (len(operands) - 2)
        out_shape = [jax.ShapeDtypeStruct((share, width), bf16)]
        next_place, final = None, 0
        if step + AHEAD < chunks:
            next_place = places[step + AHEAD]
            operands.append(in_hbm(inputs))
            in_specs.append(hbm)
            out_shape.append(pltpu.VMEM((share, width), bf16))
            scratch.append(pltpu.SemaphoreType.DMA)
        elif finished:
            final = batches
            operands += finished
            in_specs += [vmem] * len(finished)
            out_shape = [jax.ShapeDtypeStruct((batches, share, width), bf16)]
        return pl.pallas_call(
            lambda *refs: layers_kernel(sizes, step, chunks, next_place, final, *refs),
            in_specs=in_specs,
            out_specs=[vmem] * len(out_shape),
            out_shape=out_shape,
            scratch_shapes=scratch,
            compiler_params=limit,
        )(*operands)

    last = sections - 1

    def hop(step, out):
        moves = [(s, s + 1) for s in range(last) if 0 <= step - LAG * s < chunks]
        done = step - LAG * last
        if done >= 0 and places[done][1] < last:
            moves.append((last, places[done][1]))
        idle = [s for s in range(sections) if s not in [a for a, _ in moves]]
        open_ = [s for s in range(sections) if s not in [b for _, b in moves]]
        pairs = [(a * neurons + n, b * neurons + n) for a, b in moves for n in range(neurons)]
        if 0 < step <= LAG:
            idle = [s for s in idle if s in open_]
            open_ = idle
        for a, b in zip(
            [s for s in idle if s not in open_] + [s for s in idle if s in open_],
            [s for s in open_ if s not in idle] + [s for s in open_ if s in idle],
        ):
            pairs += [
                (a * neurons + n, b * neurons + (n ^ 1 if a == b else n)) for n in range(neurons)
            ]
        return lax.ppermute(out, both, pairs)

    steps = chunks + LAG * last
    own = {k: packed[len(shapes) - AHEAD + k] for k in range(AHEAD)}
    sources, sent, hops = {}, {}, {}
    finished = [None] * batches
    ended = []
    for step in range(steps):
        if step < AHEAD:
            source = own[step]
        else:
            source = sources[step]
        halo = halos[step]
        source = tie(source, *halo, *sent.get(step + 1, ()))
        ending = step == steps - 1
        if ending:
            (result,) = run(step, source, halo, finished + [jnp.stack(ended)])
            return result
        out, *following = run(step, source, halo)
        if following:
            own[step + AHEAD] = following[0]
        done = step - LAG * last
        if done < 0 or places[done][1] < last:
            hops[step] = hop(step, out)
        else:
            ended.append(out)
        coming = step + AHEAD
        if coming < steps:
            after = (out, *halos[coming - 1][1:]) if coming < steps - 1 else (out,)
            if coming < LAG:
                here = tie(own[coming], *after)
            else:
                here = tie(hops[coming - LAG], *after)
                if coming < chunks:
                    here = jnp.where(here_is[0], own[coming], here)
            sources[coming] = here
            low, high = here[:, :edge], here[:, width - edge :]
            sent[coming] = (jnp.where(even, low, high), jnp.where(even, high, low))
            which = [s for s in range(sections) if 0 <= coming - LAG * s < chunks]
            far = send_far(sent[coming][0], which)
            halos[coming] = [send_near(sent[coming][1]), far]
        back = step - 1 - LAG * last
        if back >= 0 and places[back][1] < last:
            batch, target = places[back]
            arrived = hops[step - 1]
            if finished[batch] is not None:
                arrived = jnp.where(here_is[target], arrived, finished[batch])
            finished[batch] = arrived


def solution(mesh):
    in_specs = (
        P(None, None, "neuron"),
        P("section", "neuron", None, None, None),
        P("section", "neuron"),
        P("section", None),
    )
    out_specs = P(None, "section", "neuron")
    return jax.shard_map(shards, mesh=mesh, in_specs=in_specs, out_specs=out_specs, check_vma=False)
```

```python
import jax
import jax.numpy as jnp
from jax import lax
from jax.experimental import pallas as pl
from jax.experimental.pallas import tpu as pltpu
from jax.sharding import PartitionSpec as P

HALO = 3
CEILING = 2.0
LAG = 3
AHEAD = 2


def tie(value, *after):
    return lax.optimization_barrier((value, *after))[0]


def in_hbm(value):
    return pltpu.with_memory_space_constraint(value, pltpu.HBM)


def stage_kernel(copies, bias_rows, where_ref, bias_ref, weights_ref, inputs_ref, *refs):
    outs, bias_buffer, bias_sem, sems = refs[:-3], refs[-3], refs[-2], refs[-1]
    sources = {"weights": weights_ref, "inputs": inputs_ref}

    def run(side):
        bias_copy = pltpu.make_async_copy(bias_ref, bias_buffer, bias_sem)
        bias_copy.start()
        started = []
        for k, (out, rows, name, index) in enumerate(copies[side]):
            target = outs[out].at[rows]
            started.append(pltpu.make_async_copy(sources[name].at[index], target, sems.at[k]))
            started[-1].start()
        bias_copy.wait()
        for out, row, layer, first, count, block in bias_rows[side]:
            own = bias_buffer[layer : layer + 1, first * block : (first + count) * block]
            own = own.astype(jnp.float32)
            parts = [own[:, k * block : (k + 1) * block] for k in range(count)]
            parts.append(jnp.zeros((16 - count, block), jnp.float32))
            outs[out][row : row + 16] = jnp.concatenate(parts, axis=0).astype(jnp.bfloat16)
        for copy in started:
            copy.wait()

    @pl.when(where_ref[1] == 0)
    def _():
        run(0)

    @pl.when(where_ref[1] != 0)
    def _():
        run(1)


def layers_kernel(sizes, step, chunks, next_place, final, *refs):
    layer_count, block_count, band_count, block, margin, share = sizes
    where_ref, offsets_ref, bias_ref, weights_ref = refs[:4]
    refs = refs[4:]
    table_refs, refs = refs[: 2 * (layer_count - 1)], refs[2 * (layer_count - 1) :]
    source_ref, near_ref, far_ref = refs[:3]
    refs = refs[3:]
    if next_place:
        inputs_ref, out_ref, next_ref, *buffers, sem = refs
        batch, target = next_place
        following = pltpu.make_async_copy(
            inputs_ref.at[batch, pl.ds(target * share, share)], next_ref, sem
        )
        following.start()
    elif final:
        *done_refs, last_ref, all_ref = refs[: final + 2]
        out_ref, buffers = all_ref.at[final - 1], refs[final + 2 :]
    else:
        out_ref, *buffers = refs
    even = where_ref[1] == 0
    chunk = step - LAG * where_ref[0]
    edge = margin * block
    width = block_count * block
    depth = band_count * block
    active = jnp.logical_and(chunk >= 0, chunk < chunks)

    @pl.when(active)
    def _():
        first = buffers[0]
        near, far = near_ref[...], far_ref[...]
        first[:, :edge] = jnp.where(even, far, near)
        first[:, edge + width :] = jnp.where(even, near, far)
        first[:, edge : edge + width] = source_ref[...]

        bias = bias_ref[...].astype(jnp.float32)
        for layer in range(layer_count):
            side = (layer_count - 1 - layer) * HALO
            source = buffers[layer]
            shift = [offsets_ref[layer, band] for band in range(band_count)]
            if side:
                tables = table_refs[2 * layer : 2 * layer + 2]
                last = slice(side * depth, side * depth + 16)
                sides = [table[last].astype(jnp.float32) for table in tables]
                before_bias = jnp.where(even, sides[1], sides[0])
                after_bias = jnp.where(even, sides[0], sides[1])
            for j in range(block_count + 2 * side):
                own = j - side
                x = jnp.concatenate(
                    [
                        source[:, pl.ds(pl.multiple_of((j + HALO + s) * block, block), block)]
                        for s in shift
                    ],
                    axis=1,
                )
                if own < 0:
                    k = slice(j * depth, (j + 1) * depth)
                    w = jnp.where(even, tables[1][k], tables[0][k])
                    b = before_bias[j : j + 1]
                elif own >= block_count:
                    k = own - block_count
                    b = after_bias[k : k + 1]
                    k = slice(k * depth, (k + 1) * depth)
                    w = jnp.where(even, tables[0][k], tables[1][k])
                else:
                    w = weights_ref[layer, own].reshape(depth, block)
                    b = bias[layer : layer + 1, own * block : (own + 1) * block]
                y = jnp.dot(x, w, preferred_element_type=jnp.float32) + b
                y = jnp.clip(y, 0.0, CEILING).astype(jnp.bfloat16)
                if layer < layer_count - 1:
                    buffers[layer + 1][:, j * block : (j + 1) * block] = y
                else:
                    out_ref[:, j * block : (j + 1) * block] = y

    if next_place:
        following.wait()
    if final:
        @pl.when(active)
        def _():
            for batch in range(final - 1):
                all_ref[batch] = last_ref[batch]

        @pl.when(jnp.logical_not(active))
        def _():
            for batch in range(final):
                all_ref[batch] = done_refs[batch][...]


def shards(inputs, weights, bias, offsets):
    sections = lax.axis_size("section")
    neurons = lax.axis_size("neuron")
    both = ("section", "neuron")
    section = lax.axis_index("section")
    odd = lax.axis_index("neuron") % 2
    batches, rows, width = inputs.shape
    layer_count, block_count, band_count, block, _ = weights.shape
    margin = layer_count * HALO
    edge = margin * block
    share = rows // sections
    depth = band_count * block
    places = [(batch, target) for target in range(sections) for batch in range(batches)]
    chunks = len(places)
    assert chunks <= sections * LAG and neurons % 2 == 0 and chunks > LAG

    def send_near(value):
        pairs = [
            (s * neurons + n, s * neurons + (n ^ 1))
            for s in range(sections)
            for n in range(neurons)
        ]
        return lax.ppermute(value, both, pairs)

    def send_far(value, which=range(sections)):
        pairs = []
        for s in range(sections):
            for n in range(neurons):
                other = (n + (1 if n % 2 else -1)) % neurons if s in which else n ^ 1
                pairs.append((s * neurons + n, s * neurons + other))
        return lax.ppermute(value, both, pairs)

    where = jnp.stack([section, odd]).astype(jnp.int32)
    here_is = [section == s for s in range(sections - 1)]
    even, inputs, weights, bias, offsets, where, *here_is = lax.optimization_barrier(
        (odd == 0, inputs, weights, bias, offsets, where, *here_is)
    )
    sizes = (layer_count, block_count, band_count, block, margin, share)
    smem = pl.BlockSpec(memory_space=pltpu.SMEM)
    vmem = pl.BlockSpec(memory_space=pltpu.VMEM)
    hbm = pl.BlockSpec(memory_space=pltpu.HBM)
    bf16 = jnp.bfloat16
    limit = pltpu.CompilerParams(vmem_limit_bytes=8 * 1024 * 1024)

    copies, bias_rows, shapes = [[], []], [[], []], []
    for k in range(AHEAD):
        batch, target = places[k]
        for far in (True, False):
            for parity in range(2):
                end = pl.ds(0 if far == (parity == 0) else width - edge, edge)
                index = (batch, pl.ds(target * share, share), end)
                copies[parity].append((len(shapes), pl.ds(0, share), "inputs", index))
            shapes.append((share, edge))
    for layer in range(layer_count - 1):
        side = (layer_count - 1 - layer) * HALO
        for far in (True, False):
            for parity in range(2):
                first = 0 if far == (parity == 0) else block_count - side
                index = (layer, pl.ds(first * depth, side * depth))
                copies[parity].append((len(shapes), pl.ds(0, side * depth), "weights", index))
                bias_rows[parity].append((len(shapes), side * depth, layer, first, side, block))
            shapes.append((side * depth + 16, block))
    for k in range(AHEAD):
        batch, target = places[k]
        index = (batch, pl.ds(target * share, share))
        for parity in range(2):
            copies[parity].append((len(shapes), pl.ds(0, share), "inputs", index))
        shapes.append((share, width))
    def stage(wanted, first):
        at = {k: i for i, k in enumerate(wanted)}
        my_copies = [[(at[c[0]], *c[1:]) for c in side if c[0] in at] for side in copies]
        my_rows = [[(at[c[0]], *c[1:]) for c in side if c[0] in at] for side in bias_rows]
        return pl.pallas_call(
            lambda *refs: stage_kernel(my_copies, my_rows, *refs),
            in_specs=[smem, hbm, hbm, hbm],
            out_specs=[vmem] * len(wanted),
            out_shape=[pltpu.VMEM(shapes[k], bf16) for k in wanted],
            scratch_shapes=[
                pltpu.VMEM(bias.shape, bf16),
                pltpu.SemaphoreType.DMA,
                pltpu.SemaphoreType.DMA((len(my_copies[0]),)),
            ],
            compiler_params=limit,
        )(
            tie(where, *first),
            in_hbm(bias),
            in_hbm(weights.reshape(layer_count, block_count * depth, block)),
            in_hbm(inputs),
        )

    urgent = list(range(2 * AHEAD, 2 * AHEAD + 2 * (layer_count - 1), 2))
    packed = dict(zip(urgent, stage(urgent, ())))
    others = [k for k in range(len(shapes)) if k not in urgent]
    packed.update(zip(others, stage(others, packed.values())))
    halos = {}
    for k in range(AHEAD):
        if k == 1:
            tables = []
            for layer in range(layer_count - 1):
                far = send_far(packed[2 * AHEAD + 2 * layer])
                tables += [send_near(packed[2 * AHEAD + 1 + 2 * layer]), far]
        far = send_far(packed[2 * k], [0])
        halos[k] = [send_near(packed[2 * k + 1]), far]

    def run(step, source, halo, finished=None):
        scratch = [pltpu.VMEM((share, width + 2 * edge), bf16)]
        for layer in range(1, layer_count):
            side = (layer_count - layer) * HALO
            scratch.append(pltpu.VMEM((share, width + 2 * side * block), bf16))
        operands = [where, offsets, bias, weights, *tables, source, *halo]
        in_specs = [smem, smem] + [vmem] * (len(operands) - 2)
        out_shape = [jax.ShapeDtypeStruct((share, width), bf16)]
        next_place, final = None, 0
        if step + AHEAD < chunks:
            next_place = places[step + AHEAD]
            operands.append(in_hbm(inputs))
            in_specs.append(hbm)
            out_shape.append(pltpu.VMEM((share, width), bf16))
            scratch.append(pltpu.SemaphoreType.DMA)
        elif finished:
            final = batches
            operands += finished
            in_specs += [vmem] * len(finished)
            out_shape = [jax.ShapeDtypeStruct((batches, share, width), bf16)]
        return pl.pallas_call(
            lambda *refs: layers_kernel(sizes, step, chunks, next_place, final, *refs),
            in_specs=in_specs,
            out_specs=[vmem] * len(out_shape),
            out_shape=out_shape,
            scratch_shapes=scratch,
            compiler_params=limit,
        )(*operands)

    last = sections - 1

    def hop(step, out):
        moves = [(s, s + 1) for s in range(last) if 0 <= step - LAG * s < chunks]
        done = step - LAG * last
        if done >= 0 and places[done][1] < last:
            moves.append((last, places[done][1]))
        idle = [s for s in range(sections) if s not in [a for a, _ in moves]]
        open_ = [s for s in range(sections) if s not in [b for _, b in moves]]
        pairs = [(a * neurons + n, b * neurons + n) for a, b in moves for n in range(neurons)]
        if 0 < step < LAG:
            idle = [s for s in idle if s in open_]
            open_ = idle
        for a, b in zip(
            [s for s in idle if s not in open_] + [s for s in idle if s in open_],
            [s for s in open_ if s not in idle] + [s for s in open_ if s in idle],
        ):
            pairs += [
                (a * neurons + n, b * neurons + (n ^ 1 if a == b else n)) for n in range(neurons)
            ]
        return lax.ppermute(out, both, pairs)

    steps = chunks + LAG * last
    own = {k: packed[len(shapes) - AHEAD + k] for k in range(AHEAD)}
    sources, sent, hops = {}, {}, {}
    finished = [None] * batches
    ended = []
    for step in range(steps):
        if step < AHEAD:
            source = own[step]
        else:
            source = sources[step]
        halo = halos[step]
        source = tie(source, *halo, *sent.get(step + 1, ()))
        ending = step == steps - 1
        if ending:
            (result,) = run(step, source, halo, finished + [jnp.stack(ended)])
            return result
        out, *following = run(step, source, halo)
        if following:
            own[step + AHEAD] = following[0]
        done = step - LAG * last
        if done < 0 or places[done][1] < last:
            hops[step] = hop(step, out)
        else:
            ended.append(out)
        coming = step + AHEAD
        if coming < steps:
            after = (out, *halos[coming - 1][1:]) if coming < steps - 1 else (out,)
            if coming < LAG:
                here = tie(own[coming], *after)
            else:
                here = tie(hops[coming - LAG], *after)
                if coming < chunks:
                    here = jnp.where(here_is[0], own[coming], here)
            sources[coming] = here
            low, high = here[:, :edge], here[:, width - edge :]
            sent[coming] = (jnp.where(even, low, high), jnp.where(even, high, low))
            which = [s for s in range(sections) if 0 <= coming - LAG * s < chunks]
            far = send_far(sent[coming][0], which)
            halos[coming] = [send_near(sent[coming][1]), far]
        back = step - 1 - LAG * last
        if back >= 0 and places[back][1] < last:
            batch, target = places[back]
            arrived = hops[step - 1]
            if finished[batch] is not None:
                arrived = jnp.where(here_is[target], arrived, finished[batch])
            finished[batch] = arrived


def solution(mesh):
    in_specs = (
        P(None, None, "neuron"),
        P("section", "neuron", None, None, None),
        P("section", "neuron"),
        P("section", None),
    )
    out_specs = P(None, "section", "neuron")
    return jax.shard_map(shards, mesh=mesh, in_specs=in_specs, out_specs=out_specs, check_vma=False)
```
